256 devices in a mesh: layer: 16 (over x_lo, z), latent: 16 (over x_hi, y, core).
Axes of the slice: x: 4 (x_hi: 2, x_lo: 2; x = x_hi * 2 + x_lo), y: 4, z: 8, core: 2. Of those that a mesh axis runs over, the one named last changes fastest.
Arguments:
- acts: bfloat16 [512, 16, 2304], P(None, 'layer'), may hold values from -24 to 24
- enc_weight: bfloat16 [16, 2304, 8192], P('layer', None, 'latent'), may hold values from -0.015625 to 0.015625
- dec_weight: bfloat16 [8192, 16, 2304], P('latent', 'layer'), may hold values from -0.09375 to 0.09375
- enc_bias: float32 [8192], P('latent'), may hold values from -3 to 3
- dec_bias: float32 [16, 2304], P('layer'), may hold values from -3 to 3
Outputs:
- latent_grad: float32 [512, 8192], P('layer', 'latent')
- enc_grad: bfloat16 [16, 2304, 8192], P('layer', None, 'latent')
- dec_grad: bfloat16 [8192, 16, 2304], P('latent', 'layer')
The draws below stay inside these ranges and needn't reach their ends.
All inputs are finite; a program needn't handle non-finite values.
Results may differ from the reference program's by a relative error of at most 0.012.
Values may be sent and summed in bfloat16 or wider, within the bound.
No kernel may reach another device: no remote copies, remote signals or barrier semaphores. Data moves between devices by JAX's collectives and lax.ppermute only.
A program may use at most 64 MiB of HBM per device.

```python
import math
import jax
import jax.numpy as jnp

D = 2304
F = 8192
TOKENS = 512
LAYERS = 16


def draw_acts(key, part):
    key = jax.random.fold_in(key, 11)
    key_base, key_tok = jax.random.split(key, 2)
    depth = jnp.arange(LAYERS, dtype=jnp.float32) / max(LAYERS - 1, 1)
    layer_scale = jnp.exp(depth * jnp.log(3.0)).reshape(1, LAYERS, 1)
    token_scale = jnp.exp(jax.random.uniform(key_tok, (TOKENS, 1, 1), jnp.float32, jnp.log(0.5), jnp.log(2.0)))
    base = jax.random.normal(key_base, (TOKENS, LAYERS, D), jnp.float32)
    base = jnp.clip(base, -4.0, 4.0)
    return (base * layer_scale * token_scale).astype(jnp.bfloat16)


def block_scale(stream_key, shape, pieces, smallest, largest):
    factor_of = 1.0
    for axis_at, blocks in pieces:
        heights = jax.random.uniform(jax.random.fold_in(jax.random.fold_in(stream_key, 6), axis_at), (blocks,), jnp.float32, smallest / len(pieces), largest / len(pieces))
        factor_of = factor_of * jnp.repeat(jnp.exp(heights), shape[axis_at] // blocks).reshape((-1,) + (1,) * (len(shape) - 1 - axis_at))
    return factor_of


def centred(stream_key, extent, scale, limit, cuts=(), held_as=jnp.bfloat16):
    array = jax.random.normal(stream_key, extent, jnp.float32) * scale
    if len(cuts) > 0:
        array = block_scale(stream_key, extent, cuts, -0.22, 0.18) * array
    return jnp.clip(array, min=-limit, max=limit).astype(held_as)


def setup_inputs(seed: int = 0) -> dict:
    arg_keys = jax.random.split(jax.random.key(seed), 6)
    return {
        "acts": draw_acts(jax.random.fold_in(arg_keys[5], 71), 0),
        "enc_weight": centred(arg_keys[1], (LAYERS, D, F), (LAYERS * D * 4) ** -0.5, 0.015625, ((0, 16), (2, 16))),
        "dec_weight": centred(arg_keys[2], (F, LAYERS, D), (F // 2) ** -0.5, 0.09375, ((0, 16), (1, 16))),
        "enc_bias": centred(arg_keys[3], (F,), 0.5, 3.0, ((0, 16),), jnp.float32),
        "dec_bias": centred(arg_keys[4], (LAYERS, D), 0.5, 3.0, ((0, 16),), jnp.float32),
    }


def reference(acts, enc_weight, dec_weight, enc_bias, dec_bias):
    flat = acts.reshape(TOKENS, LAYERS * D)
    enc_flat = enc_weight.reshape(LAYERS * D, F)
    dec_flat = dec_weight.reshape(F, LAYERS * D)
    pre = jnp.dot(flat, enc_flat, preferred_element_type=jnp.float32) + enc_bias[None, :]
    latents = jnp.maximum(pre, 0.0).astype(jnp.bfloat16)
    recon = jnp.dot(latents, dec_flat, preferred_element_type=jnp.float32) + dec_bias.reshape(1, LAYERS * D)
    err_grad = ((recon - flat.astype(jnp.float32)) / math.sqrt(TOKENS)).astype(jnp.bfloat16)
    latent_grad = jnp.dot(err_grad, dec_flat.T, preferred_element_type=jnp.float32)
    grad_pre = jnp.where(pre > 0, latent_grad, jnp.float32(0.0)).astype(jnp.bfloat16)
    enc_grad = jnp.dot(flat.T, grad_pre, preferred_element_type=jnp.float32)
    dec_grad = jnp.dot(latents.T, err_grad, preferred_element_type=jnp.float32)
    return (latent_grad, enc_grad.astype(jnp.bfloat16).reshape(LAYERS, D, F), dec_grad.astype(jnp.bfloat16).reshape(F, LAYERS, D))
```

```python
import math

import jax
import jax.numpy as jnp
from jax import lax
from jax.sharding import PartitionSpec as P

F32 = jnp.float32
BF16 = jnp.bfloat16
CORE_SWAP = [(i, i ^ 1) for i in range(16)]
CHIP_GROUPS = [list(range(c, 16, 2)) for c in range(2)]


def spread(block, axis, groups=None, count=16):
    copies = jnp.broadcast_to(block[None], (count,) + block.shape)
    return lax.all_to_all(copies, axis, 0, 0, axis_index_groups=groups)


def local(acts, enc_weight, dec_weight, enc_bias, dec_bias):
    tokens, layers_here, width = acts.shape
    local_latents = enc_weight.shape[2]
    flat = acts.reshape(tokens, width)
    enc = enc_weight.reshape(width, local_latents)
    dec = dec_weight.reshape(local_latents, width)
    rows = tokens // 16
    half = tokens // 2
    core = lax.axis_index("latent") % 2
    chip = lax.axis_index("latent") // 2
    own_half = core * half
    other_half = (1 - core) * half

    partial_pre = jnp.dot(flat, enc, preferred_element_type=F32)
    parts = lax.all_to_all(partial_pre.reshape(16, rows, local_latents), "layer", 0, 0)
    own_pre = jnp.sum(parts, axis=0) + enc_bias[None, :]
    own_latents = jnp.maximum(own_pre, 0.0).astype(BF16)
    latents = spread(own_latents, "layer").reshape(tokens, local_latents)

    send = jnp.dot(
        lax.dynamic_slice_in_dim(latents, other_half, half, 0), dec, preferred_element_type=F32
    ).astype(BF16)
    received = lax.ppermute(send, "latent", CORE_SWAP)
    kept = jnp.dot(
        lax.dynamic_slice_in_dim(latents, own_half, half, 0), dec, preferred_element_type=F32
    )
    pair = (kept + received.astype(F32)).astype(BF16)
    shares = lax.all_to_all(
        pair.reshape(8, rows, width), "latent", 0, 0, axis_index_groups=CHIP_GROUPS
    )
    recon = jnp.sum(shares.astype(F32), axis=0) + dec_bias
    acts_rows = lax.dynamic_slice_in_dim(flat, own_half + chip * rows, rows, 0).astype(F32)
    err_rows = ((recon - acts_rows) / math.sqrt(tokens)).astype(BF16)
    err_own = spread(err_rows, "latent", CHIP_GROUPS, 8).reshape(half, width)
    err_other = lax.ppermute(err_own, "latent", CORE_SWAP)
    err = jnp.where(
        core == 0,
        jnp.concatenate([err_own, err_other], 0),
        jnp.concatenate([err_other, err_own], 0),
    )

    back = lax.dot_general(err, dec, (((1,), (1,)), ((), ())), preferred_element_type=F32)
    back_parts = lax.all_to_all(
        back.astype(BF16).reshape(16, rows, local_latents), "layer", 0, 0
    )
    latent_grad = jnp.sum(back_parts.astype(F32), axis=0)
    own_grad_pre = jnp.where(own_pre > 0, latent_grad, 0.0).astype(BF16)
    grad_pre = spread(own_grad_pre, "layer").reshape(tokens, local_latents)

    dec_grad = lax.dot_general(
        latents, err, (((0,), (0,)), ((), ())), preferred_element_type=F32
    ).astype(BF16)
    enc_grad = lax.dot_general(
        flat, grad_pre, (((0,), (0,)), ((), ())), preferred_element_type=F32
    ).astype(BF16)
    return (
        latent_grad,
        enc_grad.reshape(layers_here, width, local_latents),
        dec_grad.reshape(local_latents, layers_here, width),
    )


def solution(mesh):
    in_specs = (
        P(None, "layer", None),
        P("layer", None, "latent"),
        P("latent", "layer", None),
        P("latent"),
        P("layer", None),
    )
    out_specs = (P("layer", "latent"), P("layer", None, "latent"), P("latent", "layer", None))
    return jax.shard_map(local, mesh=mesh, in_specs=in_specs, out_specs=out_specs, check_vma=False)
```

```python
import math

import jax
import jax.numpy as jnp
from jax import lax
from jax.experimental import pallas as pl
from jax.experimental.pallas import tpu as pltpu
from jax.sharding import PartitionSpec as P

F32 = jnp.float32
BF16 = jnp.bfloat16
CORE_SWAP = [(i, i ^ 1) for i in range(16)]
CHIP_GROUPS = [list(range(c, 16, 2)) for c in range(2)]


Z_UP = [(x * 8 + z, x * 8 + (z + 1) % 8) for x in range(2) for z in range(8)]
Z_DOWN = [(b, a) for a, b in Z_UP]
X_NEXT = [(i, (i + 8) % 16) for i in range(16)]


def spread(block, axis, groups=None, count=16):
    copies = jnp.broadcast_to(block[None], (count,) + block.shape)
    return lax.all_to_all(copies, axis, 0, 0, axis_index_groups=groups)


def matmul_kernel(left_ref, right_ref, out_ref):
    out_ref[...] = jnp.dot(
        left_ref[...], right_ref[...], preferred_element_type=F32
    ).astype(out_ref.dtype)


def matmul(left, right, block):
    rows, depth = left.shape
    cols = right.shape[1]
    return pl.pallas_call(
        matmul_kernel,
        out_shape=jax.ShapeDtypeStruct((rows, cols), BF16),
        grid=(rows // block,),
        in_specs=[
            pl.BlockSpec((block, depth), lambda i: (i, 0)),
            pl.BlockSpec((depth, cols), lambda i: (0, 0)),
        ],
        out_specs=pl.BlockSpec((block, cols), lambda i: (i, 0)),
        compiler_params=pltpu.CompilerParams(vmem_limit_bytes=16 * 1024 * 1024),
        cost_estimate=pl.CostEstimate(
            flops=2 * rows * depth * cols,
            bytes_accessed=2 * (rows * depth + depth * cols + rows * cols),
            transcendentals=0,
        ),
    )(left, right)


def local(acts, enc_weight, dec_weight, enc_bias, dec_bias):
    tokens, layers_here, width = acts.shape
    local_latents = enc_weight.shape[2]
    flat = acts.reshape(tokens, width)
    enc = enc_weight.reshape(width, local_latents)
    dec = dec_weight.reshape(local_latents, width)
    rows = tokens // 16
    half = tokens // 2
    core = lax.axis_index("latent") % 2
    chip = lax.axis_index("latent") // 2
    own_half = core * half
    other_half = (1 - core) * half

    layer_at = lax.axis_index("layer")
    x_lo = layer_at // 8
    z = layer_at % 8
    tall = flat.reshape(2, 8, rows, width)

    def partial(step):
        block = lax.dynamic_index_in_dim(tall, (z + step) % 8, 1, keepdims=False)
        return jnp.dot(block.reshape(2 * rows, width), enc, preferred_element_type=F32)

    up, down = partial(4), partial(-3)
    up, down = lax.ppermute(up, "layer", Z_UP), lax.ppermute(down, "layer", Z_DOWN)
    up, down = up + partial(3), down + partial(-2)
    up, down = lax.ppermute(up, "layer", Z_UP), lax.ppermute(down, "layer", Z_DOWN)
    up, down = up + partial(2), down + partial(-1)
    up, down = lax.ppermute(up, "layer", Z_UP), lax.ppermute(down, "layer", Z_DOWN)
    own = partial(0)
    up = lax.ppermute(up + partial(1), "layer", Z_UP)
    column = (up + (down + own)).reshape(2, rows, local_latents)
    kept_column = lax.dynamic_index_in_dim(column, x_lo, 0, keepdims=False)
    sent_column = lax.dynamic_index_in_dim(column, 1 - x_lo, 0, keepdims=False)
    own_pre = kept_column + lax.ppermute(sent_column, "layer", X_NEXT) + enc_bias[None, :]
    own_latents = jnp.maximum(own_pre, 0.0).astype(BF16)
    latents = spread(own_latents, "layer").reshape(tokens, local_latents)

    send = jnp.dot(
        lax.dynamic_slice_in_dim(latents, other_half, half, 0), dec, preferred_element_type=F32
    ).astype(BF16)
    received = lax.ppermute(send, "latent", CORE_SWAP)
    kept = jnp.dot(
        lax.dynamic_slice_in_dim(latents, own_half, half, 0), dec, preferred_element_type=F32
    )
    pair = (kept + received.astype(F32)).astype(BF16)
    shares = lax.all_to_all(
        pair.reshape(8, rows, width), "latent", 0, 0, axis_index_groups=CHIP_GROUPS
    )
    recon = jnp.sum(shares.astype(F32), axis=0) + dec_bias
    acts_rows = lax.dynamic_slice_in_dim(flat, own_half + chip * rows, rows, 0).astype(F32)
    err_rows = ((recon - acts_rows) / math.sqrt(tokens)).astype(BF16)
    err_own = spread(err_rows, "latent", CHIP_GROUPS, 8).reshape(half, width)
    err_other = lax.ppermute(err_own, "latent", CORE_SWAP)
    err = jnp.where(
        core == 0,
        jnp.concatenate([err_own, err_other], 0),
        jnp.concatenate([err_other, err_own], 0),
    )

    back = lax.dot_general(err, dec, (((1,), (1,)), ((), ())), preferred_element_type=F32)
    back_parts = lax.all_to_all(
        back.astype(BF16).reshape(16, rows, local_latents), "layer", 0, 0
    )
    latent_grad = jnp.sum(back_parts.astype(F32), axis=0)
    own_grad_pre = jnp.where(own_pre > 0, latent_grad, 0.0).astype(BF16)
    grad_pre = spread(own_grad_pre, "layer").reshape(tokens, local_latents)

    dec_grad = lax.dot_general(
        latents, err, (((0,), (0,)), ((), ())), preferred_element_type=F32
    ).astype(BF16)
    enc_grad = matmul(flat.T, grad_pre, 384)
    return (
        latent_grad,
        enc_grad.reshape(layers_here, width, local_latents),
        dec_grad.reshape(local_latents, layers_here, width),
    )


def solution(mesh):
    in_specs = (
        P(None, "layer", None),
        P("layer", None, "latent"),
        P("latent", "layer", None),
        P("latent"),
        P("layer", None),
    )
    out_specs = (P("layer", "latent"), P("layer", None, "latent"), P("latent", "layer", None))
    return jax.shard_map(local, mesh=mesh, in_specs=in_specs, out_specs=out_specs, check_vma=False)
```

```python
import functools
import math

import jax
import jax.numpy as jnp
from jax import lax
from jax.experimental import pallas as pl
from jax.experimental.pallas import tpu as pltpu
from jax.sharding import PartitionSpec as P

F32 = jnp.float32
BF16 = jnp.bfloat16
CORE_SWAP = [(i, i ^ 1) for i in range(16)]
CHIP_GROUPS = [list(range(c, 16, 2)) for c in range(2)]


Z_UP = [(x * 8 + z, x * 8 + (z + 1) % 8) for x in range(2) for z in range(8)]
Z_DOWN = [(b, a) for a, b in Z_UP]
X_NEXT = [(i, (i + 8) % 16) for i in range(16)]


def spread(block, axis, groups=None, count=16):
    copies = jnp.broadcast_to(block[None], (count,) + block.shape)
    return lax.all_to_all(copies, axis, 0, 0, axis_index_groups=groups)


SMALL = pl.BlockSpec(memory_space=pltpu.SMEM)
LARGE = pl.BlockSpec(memory_space=pl.ANY)
STORED = pl.BlockSpec(memory_space=pltpu.HBM)
NT = (((1,), (1,)), ((), ()))
PIECES = 3


def shape(dims, dtype):
    return jax.ShapeDtypeStruct(dims, dtype)


def whole(like):
    if like.shape == (1,):
        return SMALL
    return pl.BlockSpec(like.shape, lambda i: (0,) * len(like.shape))


def simple(kernel, out_shape, flops, moved, *operands):
    specs = [whole(operand) for operand in operands]
    return call(kernel, out_shape, whole(out_shape), specs, [], flops, moved, *operands)


def call(kernel, out_shape, out_spec, specs, scratch, flops, moved, *operands):
    return pl.pallas_call(
        kernel,
        out_shape=out_shape,
        grid=(1,),
        in_specs=specs,
        out_specs=out_spec,
        scratch_shapes=scratch,
        compiler_params=pltpu.CompilerParams(vmem_limit_bytes=20 * 1024 * 1024),
        cost_estimate=pl.CostEstimate(flops=flops, bytes_accessed=moved, transcendentals=0),
    )(*operands)


def error_kernel(shares_ref, bias_ref, acts_ref, copies_ref, *, scale):
    recon = shares_ref[0].astype(F32)
    for i in range(1, shares_ref.shape[0]):
        recon += shares_ref[i].astype(F32)
    err = (recon + bias_ref[...] - acts_ref[...].astype(F32)) / scale
    err = err.astype(BF16)
    for i in range(copies_ref.shape[0]):
        copies_ref[i] = err


def half_of(ref, which):
    rows = ref.shape[0] // 2
    return ref[pl.ds(pl.multiple_of(which * rows, rows), rows), :]


def send_kernel(core_ref, latents_ref, dec_ref, out_ref):
    left = half_of(latents_ref, 1 - core_ref[0])
    out_ref[...] = jnp.dot(left, dec_ref[...], preferred_element_type=F32).astype(BF16)


def keep_kernel(core_ref, latents_ref, dec_ref, received_ref, out_ref):
    left = half_of(latents_ref, core_ref[0])
    total = jnp.dot(left, dec_ref[...], preferred_element_type=F32)
    out_ref[...] = (total + received_ref[...].astype(F32)).astype(BF16)


def back_own_kernel(err_ref, dec_ref, out_ref):
    out_ref[...] = lax.dot_general(
        err_ref[...], dec_ref[...], NT, preferred_element_type=F32
    ).astype(BF16)


def back_kernel(core_ref, err_ref, dec_ref, own_ref, out_ref):
    half = err_ref.shape[0]
    core = core_ref[0]
    other = lax.dot_general(err_ref[...], dec_ref[...], NT, preferred_element_type=F32)
    out_ref[pl.ds(pl.multiple_of(core * half, half), half), :] = own_ref[...]
    out_ref[pl.ds(pl.multiple_of((1 - core) * half, half), half), :] = other.astype(BF16)


def enc_kernel(acts_ref, grad_ref, out_ref, acts_buf, out_buf, sems):
    step = acts_ref.shape[0] // PIECES
    rows = [slice(i * step, (i + 1) * step) for i in range(PIECES)]
    loads = [
        pltpu.make_async_copy(acts_ref.at[r], acts_buf.at[r], sems.at[0, i])
        for i, r in enumerate(rows)
    ]
    for load in loads:
        load.start()
    grad = grad_ref[...]
    stores = []
    for i, r in enumerate(rows):
        loads[i].wait()
        out_buf[r] = jnp.dot(acts_buf[r], grad, preferred_element_type=F32).astype(BF16)
        stores.append(pltpu.make_async_copy(out_buf.at[r], out_ref.at[r], sems.at[1, i]))
        stores[-1].start()
    for store in stores:
        store.wait()


def local(acts, enc_weight, dec_weight, enc_bias, dec_bias):
    tokens, layers_here, width = acts.shape
    local_latents = enc_weight.shape[2]
    flat = acts.reshape(tokens, width)
    enc = enc_weight.reshape(width, local_latents)
    dec = dec_weight.reshape(local_latents, width)
    rows = tokens // 16
    half = tokens // 2
    core = lax.axis_index("latent") % 2
    chip = lax.axis_index("latent") // 2
    core_at = core.reshape(1)
    own_half = core * half
    other_half = (1 - core) * half

    layer_at = lax.axis_index("layer")
    x_lo = layer_at // 8
    z = layer_at % 8
    tall = flat.reshape(2, 8, rows, width)

    def partial(step):
        block = lax.dynamic_index_in_dim(tall, (z + step) % 8, 1, keepdims=False)
        return jnp.dot(block.reshape(2 * rows, width), enc, preferred_element_type=F32)

    up, down = partial(4), partial(-3)
    up, down, tall = lax.optimization_barrier((up, down, tall))
    up, down = lax.ppermute(up, "layer", Z_UP), lax.ppermute(down, "layer", Z_DOWN)
    up, down = up + partial(3), down + partial(-2)
    up, down = lax.ppermute(up, "layer", Z_UP), lax.ppermute(down, "layer", Z_DOWN)
    up, down = up + partial(2), down + partial(-1)
    up, down = lax.ppermute(up, "layer", Z_UP), lax.ppermute(down, "layer", Z_DOWN)
    own = partial(0)
    up = lax.ppermute(up + partial(1), "layer", Z_UP)
    column = (up + (down + own)).reshape(2, rows, local_latents)
    kept_column = lax.dynamic_index_in_dim(column, x_lo, 0, keepdims=False)
    sent_column = lax.dynamic_index_in_dim(column, 1 - x_lo, 0, keepdims=False)
    own_pre = kept_column + lax.ppermute(sent_column, "layer", X_NEXT) + enc_bias[None, :]
    own_latents = jnp.maximum(own_pre, 0.0).astype(BF16)
    latents = spread(own_latents, "layer").reshape(tokens, local_latents)

    acts_rows = lax.dynamic_slice_in_dim(flat, own_half + chip * rows, rows, 0)
    latents, acts_t, acts_rows = lax.optimization_barrier((latents, flat.T, acts_rows))
    flops = 2 * half * local_latents * width
    moved = 2 * (local_latents + half) * width
    halves = shape((half, width), BF16)
    send = simple(send_kernel, halves, flops, moved, core_at, latents, dec)
    received = lax.ppermute(send, "latent", CORE_SWAP)
    chip_sum = simple(keep_kernel, halves, flops, moved, core_at, latents, dec, received)
    shares = lax.all_to_all(
        chip_sum.reshape(8, rows, width), "latent", 0, 0, axis_index_groups=CHIP_GROUPS
    )
    copies = shape((8, rows, width), BF16)
    err_copies = simple(
        functools.partial(error_kernel, scale=math.sqrt(tokens)),
        copies,
        12 * rows * width,
        36 * rows * width,
        shares,
        dec_bias,
        acts_rows,
    )
    err_own = lax.all_to_all(err_copies, "latent", 0, 0, axis_index_groups=CHIP_GROUPS)
    err_own = err_own.reshape(half, width)

    err_other = lax.ppermute(err_own, "latent", CORE_SWAP)
    back = simple(
        back_own_kernel, shape((half, local_latents), BF16), flops, moved, err_own, dec
    )
    back = simple(
        back_kernel,
        shape((tokens, local_latents), BF16),
        flops,
        moved,
        core_at,
        err_other,
        dec,
        back,
    )
    err = jnp.where(
        core == 0,
        jnp.concatenate([err_own, err_other], 0),
        jnp.concatenate([err_other, err_own], 0),
    )
    back_parts = lax.all_to_all(
        back.reshape(16, rows, local_latents), "layer", 0, 0
    )
    latent_grad = jnp.sum(back_parts.astype(F32), axis=0)
    own_grad_pre = jnp.where(own_pre > 0, latent_grad, 0.0).astype(BF16)
    latents_late, err_late, latent_grad = lax.optimization_barrier((latents, err, latent_grad))
    dec_grad = lax.dot_general(
        latents_late, err_late, (((0,), (0,)), ((), ())), preferred_element_type=F32
    ).astype(BF16)
    grad_pre = spread(own_grad_pre, "layer").reshape(tokens, local_latents)
    enc_grad = call(
        enc_kernel,
        shape((width, local_latents), BF16),
        STORED,
        [LARGE, whole(grad_pre)],
        [
            pltpu.VMEM((width, tokens), BF16),
            pltpu.VMEM((width, local_latents), BF16),
            pltpu.SemaphoreType.DMA((2, PIECES)),
        ],
        2 * tokens * width * local_latents,
        3 * moved,
        acts_t,
        grad_pre,
    )
    return (
        latent_grad,
        enc_grad.reshape(layers_here, width, local_latents),
        dec_grad.reshape(local_latents, layers_here, width),
    )


def solution(mesh):
    in_specs = (
        P(None, "layer", None),
        P("layer", None, "latent"),
        P("latent", "layer", None),
        P("latent"),
        P("layer", None),
    )
    out_specs = (P("layer", "latent"), P("layer", None, "latent"), P("latent", "layer", None))
    return jax.shard_map(local, mesh=mesh, in_specs=in_specs, out_specs=out_specs, check_vma=False)
```

```python
import functools
import math

import jax
import jax.numpy as jnp
from jax import lax
from jax.experimental import pallas as pl
from jax.experimental.pallas import tpu as pltpu
from jax.sharding import PartitionSpec as P

F32 = jnp.float32
BF16 = jnp.bfloat16
CORE_SWAP = [(i, i ^ 1) for i in range(16)]
CHIP_GROUPS = [list(range(c, 16, 2)) for c in range(2)]


Z_UP = [(x * 8 + z, x * 8 + (z + 1) % 8) for x in range(2) for z in range(8)]
Z_DOWN = [(b, a) for a, b in Z_UP]
Z_ACROSS = [(a, b ^ 8) for a, b in Z_UP]
X_NEXT = [(i, (i + 8) % 16) for i in range(16)]


def spread(block, axis, groups=None, count=16):
    copies = jnp.broadcast_to(block[None], (count,) + block.shape)
    return lax.all_to_all(copies, axis, 0, 0, axis_index_groups=groups)


SMALL = pl.BlockSpec(memory_space=pltpu.SMEM)
STORED = pl.BlockSpec(memory_space=pltpu.HBM)
NT = (((1,), (1,)), ((), ()))
PIECES = 3


def shape(dims, dtype):
    return jax.ShapeDtypeStruct(dims, dtype)


def whole(like):
    if like.shape == (1,):
        return SMALL
    return pl.BlockSpec(like.shape, lambda i: (0,) * len(like.shape))


def simple(kernel, out_shape, flops, moved, *operands):
    specs = [whole(operand) for operand in operands]
    return call(kernel, out_shape, whole(out_shape), specs, [], flops, moved, *operands)


def call(kernel, out_shape, out_spec, specs, scratch, flops, moved, *operands, room=20):
    return pl.pallas_call(
        kernel,
        out_shape=out_shape,
        grid=(1,),
        in_specs=specs,
        out_specs=out_spec,
        scratch_shapes=scratch,
        compiler_params=pltpu.CompilerParams(vmem_limit_bytes=room * 1024 * 1024),
        cost_estimate=pl.CostEstimate(flops=flops, bytes_accessed=moved, transcendentals=0),
    )(*operands)


def error_kernel(shares_ref, bias_ref, acts_ref, copies_ref, *, scale):
    recon = shares_ref[0].astype(F32)
    for i in range(1, shares_ref.shape[0]):
        recon += shares_ref[i].astype(F32)
    err = (recon + bias_ref[...] - acts_ref[...].astype(F32)) / scale
    err = err.astype(BF16)
    for i in range(copies_ref.shape[0]):
        copies_ref[i] = err


def half_of(ref, which):
    rows = ref.shape[0] // 2
    return ref[pl.ds(pl.multiple_of(which * rows, rows), rows), :]


def send_kernel(core_ref, latents_ref, dec_ref, out_ref):
    left = half_of(latents_ref, 1 - core_ref[0])
    out_ref[...] = jnp.dot(left, dec_ref[...], preferred_element_type=F32).astype(BF16)


def keep_kernel(core_ref, latents_ref, dec_ref, received_ref, out_ref):
    left = half_of(latents_ref, core_ref[0])
    total = jnp.dot(left, dec_ref[...], preferred_element_type=F32)
    out_ref[...] = (total + received_ref[...].astype(F32)).astype(BF16)


def back_own_kernel(err_ref, dec_ref, out_ref):
    out_ref[...] = lax.dot_general(
        err_ref[...], dec_ref[...], NT, preferred_element_type=F32
    ).astype(BF16)


def back_kernel(core_ref, err_ref, dec_ref, own_ref, out_ref):
    half = err_ref.shape[0]
    core = core_ref[0]
    other = lax.dot_general(err_ref[...], dec_ref[...], NT, preferred_element_type=F32)
    out_ref[pl.ds(pl.multiple_of(core * half, half), half), :] = own_ref[...]
    out_ref[pl.ds(pl.multiple_of((1 - core) * half, half), half), :] = other.astype(BF16)


def enc_kernel(acts_ref, grad_ref, out_ref):
    out_ref[...] = jnp.dot(
        acts_ref[...], grad_ref[...], preferred_element_type=F32
    ).astype(BF16)


def local(acts, enc_weight, dec_weight, enc_bias, dec_bias):
    tokens, layers_here, width = acts.shape
    local_latents = enc_weight.shape[2]
    flat = acts.reshape(tokens, width)
    enc = enc_weight.reshape(width, local_latents)
    dec = dec_weight.reshape(local_latents, width)
    rows = tokens // 16
    half = tokens // 2
    core = lax.axis_index("latent") % 2
    chip = lax.axis_index("latent") // 2
    core_at = core.reshape(1)
    own_half = core * half
    other_half = (1 - core) * half

    layer_at = lax.axis_index("layer")
    x_lo = layer_at // 8
    z = layer_at % 8
    tall = flat.reshape(2, 8, rows, width)

    def partial(step):
        block = lax.dynamic_index_in_dim(tall, (z + step) % 8, 1, keepdims=False)
        return jnp.dot(block.reshape(2 * rows, width), enc, preferred_element_type=F32)

    up, down = partial(4), partial(-3)
    up, down, tall = lax.optimization_barrier((up, down, tall))
    up, down = lax.ppermute(up, "layer", Z_UP), lax.ppermute(down, "layer", Z_DOWN)
    up, down = up + partial(3), down + partial(-2)
    up, down = lax.ppermute(up, "layer", Z_UP), lax.ppermute(down, "layer", Z_DOWN)
    up, down = up + partial(2), down + partial(-1)
    up, down = lax.ppermute(up, "layer", Z_UP), lax.ppermute(down, "layer", Z_DOWN)
    up = (up + partial(1)).reshape(2, rows, local_latents)
    down = (down + partial(0)).reshape(2, rows, local_latents)

    def column(x, at):
        return lax.dynamic_index_in_dim(x, at, 0, keepdims=False)

    arrived = (
        lax.ppermute(column(up, 1 - x_lo), "layer", Z_ACROSS),
        lax.ppermute(column(up, x_lo), "layer", Z_UP),
        lax.ppermute(column(down, 1 - x_lo), "layer", X_NEXT),
    )
    own_pre = column(down, x_lo) + sum(arrived) + enc_bias[None, :]
    own_latents = jnp.maximum(own_pre, 0.0).astype(BF16)
    latents = spread(own_latents, "layer").reshape(tokens, local_latents)

    acts_rows = lax.dynamic_slice_in_dim(flat, own_half + chip * rows, rows, 0)
    latents, acts_t, acts_rows = lax.optimization_barrier((latents, flat.T, acts_rows))
    flops = 2 * half * local_latents * width
    moved = 2 * (local_latents + half) * width
    halves = shape((half, width), BF16)
    send = simple(send_kernel, halves, flops, moved, core_at, latents, dec)
    received = lax.ppermute(send, "latent", CORE_SWAP)
    chip_sum = simple(keep_kernel, halves, flops, moved, core_at, latents, dec, received)
    shares = lax.all_to_all(
        chip_sum.reshape(8, rows, width), "latent", 0, 0, axis_index_groups=CHIP_GROUPS
    )
    copies = shape((8, rows, width), BF16)
    err_copies = simple(
        functools.partial(error_kernel, scale=math.sqrt(tokens)),
        copies,
        12 * rows * width,
        36 * rows * width,
        shares,
        dec_bias,
        acts_rows,
    )
    err_own = lax.all_to_all(err_copies, "latent", 0, 0, axis_index_groups=CHIP_GROUPS)
    err_own = err_own.reshape(half, width)

    err_other = lax.ppermute(err_own, "latent", CORE_SWAP)
    back = simple(
        back_own_kernel, shape((half, local_latents), BF16), flops, moved, err_own, dec
    )
    back = simple(
        back_kernel,
        shape((tokens, local_latents), BF16),
        flops,
        moved,
        core_at,
        err_other,
        dec,
        back,
    )
    err = jnp.where(
        core == 0,
        jnp.concatenate([err_own, err_other], 0),
        jnp.concatenate([err_other, err_own], 0),
    )
    back_parts = lax.all_to_all(
        back.reshape(16, rows, local_latents), "layer", 0, 0
    )
    latent_grad = jnp.sum(back_parts.astype(F32), axis=0)
    own_grad_pre = jnp.where(own_pre > 0, latent_grad, 0.0).astype(BF16)
    dec_grad = lax.dot_general(
        latents, err, (((0,), (0,)), ((), ())), preferred_element_type=F32
    ).astype(BF16)
    own_grad_pre, dec_grad = lax.optimization_barrier((own_grad_pre, dec_grad))
    grad_pre = spread(own_grad_pre, "layer").reshape(tokens, local_latents)
    enc_grad = pl.pallas_call(
        enc_kernel,
        out_shape=shape((width, local_latents), BF16),
        grid=(2,),
        in_specs=[pl.BlockSpec((width // 2, tokens), lambda i: (i, 0)), whole(grad_pre)],
        out_specs=pl.BlockSpec((width // 2, local_latents), lambda i: (i, 0)),
        compiler_params=pltpu.CompilerParams(vmem_limit_bytes=16 * 1024 * 1024),
        cost_estimate=pl.CostEstimate(
            flops=2 * tokens * width * local_latents, bytes_accessed=3 * moved, transcendentals=0
        ),
    )(acts_t, grad_pre)
    return (
        latent_grad,
        enc_grad.reshape(layers_here, width, local_latents),
        dec_grad.reshape(local_latents, layers_here, width),
    )


def solution(mesh):
    in_specs = (
        P(None, "layer", None),
        P("layer", None, "latent"),
        P("latent", "layer", None),
        P("latent"),
        P("layer", None),
    )
    out_specs = (P("layer", "latent"), P("layer", None, "latent"), P("latent", "layer", None))
    return jax.shard_map(local, mesh=mesh, in_specs=in_specs, out_specs=out_specs, check_vma=False)
```

```python
import functools
import math

import jax
import jax.numpy as jnp
from jax import lax
from jax.experimental import pallas as pl
from jax.experimental.pallas import tpu as pltpu
from jax.sharding import PartitionSpec as P

F32 = jnp.float32
BF16 = jnp.bfloat16
CORE_SWAP = [(i, i ^ 1) for i in range(16)]
CHIP_GROUPS = [list(range(c, 16, 2)) for c in range(2)]


Z_UP = [(x * 8 + z, x * 8 + (z + 1) % 8) for x in range(2) for z in range(8)]
Z_DOWN = [(b, a) for a, b in Z_UP]
Z_ACROSS = [(a, b ^ 8) for a, b in Z_UP]
X_NEXT = [(i, (i + 8) % 16) for i in range(16)]


def spread(block, axis, groups=None, count=16):
    copies = jnp.broadcast_to(block[None], (count,) + block.shape)
    return lax.all_to_all(copies, axis, 0, 0, axis_index_groups=groups)


SMALL = pl.BlockSpec(memory_space=pltpu.SMEM)
NT = (((1,), (1,)), ((), ()))
TN = (((0,), (0,)), ((), ()))


def shape(dims, dtype):
    return jax.ShapeDtypeStruct(dims, dtype)


def whole(like):
    if like.shape == (1,):
        return SMALL
    return pl.BlockSpec(like.shape, lambda i: (0,) * len(like.shape))


def simple(kernel, out_shape, flops, moved, *operands):
    specs = [whole(operand) for operand in operands]
    return call(kernel, out_shape, whole(out_shape), specs, flops, moved, *operands)


def call(kernel, out_shape, out_spec, specs, flops, moved, *operands, steps=1):
    return pl.pallas_call(
        kernel,
        out_shape=out_shape,
        grid=(steps,),
        in_specs=specs,
        out_specs=out_spec,
        compiler_params=pltpu.CompilerParams(vmem_limit_bytes=20 * 1024 * 1024),
        cost_estimate=pl.CostEstimate(flops=flops, bytes_accessed=moved, transcendentals=0),
    )(*operands)


def error_kernel(shares_ref, bias_ref, acts_ref, copies_ref, *, scale):
    recon = shares_ref[0].astype(F32)
    for i in range(1, shares_ref.shape[0]):
        recon += shares_ref[i].astype(F32)
    err = (recon + bias_ref[...] - acts_ref[...].astype(F32)) / scale
    err = err.astype(BF16)
    for i in range(copies_ref.shape[0]):
        copies_ref[i] = err


def half_of(ref, which):
    rows = ref.shape[0] // 2
    return ref[pl.ds(pl.multiple_of(which * rows, rows), rows), :]


def send_kernel(core_ref, latents_ref, dec_ref, out_ref):
    left = half_of(latents_ref, 1 - core_ref[0])
    out_ref[...] = jnp.dot(left, dec_ref[...], preferred_element_type=F32).astype(BF16)


def keep_kernel(core_ref, latents_ref, dec_ref, received_ref, out_ref):
    left = half_of(latents_ref, core_ref[0])
    total = jnp.dot(left, dec_ref[...], preferred_element_type=F32)
    out_ref[...] = (total + received_ref[...].astype(F32)).astype(BF16)


def back_own_kernel(err_ref, dec_ref, out_ref):
    out_ref[...] = lax.dot_general(
        err_ref[...], dec_ref[...], NT, preferred_element_type=F32
    ).astype(BF16)


def back_kernel(core_ref, err_ref, dec_ref, own_ref, out_ref):
    half = err_ref.shape[0]
    core = core_ref[0]
    other = lax.dot_general(err_ref[...], dec_ref[...], NT, preferred_element_type=F32)
    out_ref[pl.ds(pl.multiple_of(core * half, half), half), :] = own_ref[...]
    out_ref[pl.ds(pl.multiple_of((1 - core) * half, half), half), :] = other.astype(BF16)


def dec_kernel(core_ref, latents_ref, own_ref, other_ref, out_ref):
    core = core_ref[0]
    total = lax.dot_general(
        half_of(latents_ref, core), own_ref[...], TN, preferred_element_type=F32
    )
    total += lax.dot_general(
        half_of(latents_ref, 1 - core), other_ref[...], TN, preferred_element_type=F32
    )
    out_ref[...] = total.astype(BF16)


def enc_kernel(acts_ref, grad_ref, out_ref):
    out_ref[...] = jnp.dot(
        acts_ref[...], grad_ref[...], preferred_element_type=F32
    ).astype(BF16)


def local(acts, enc_weight, dec_weight, enc_bias, dec_bias):
    tokens, layers_here, width = acts.shape
    local_latents = enc_weight.shape[2]
    flat = acts.reshape(tokens, width)
    enc = enc_weight.reshape(width, local_latents)
    dec = dec_weight.reshape(local_latents, width)
    rows = tokens // 16
    half = tokens // 2
    core = lax.axis_index("latent") % 2
    chip = lax.axis_index("latent") // 2
    core_at = core.reshape(1)
    own_half = core * half
    other_half = (1 - core) * half

    layer_at = lax.axis_index("layer")
    x_lo = layer_at // 8
    z = layer_at % 8
    tall = flat.reshape(2, 8, rows, width)

    def partial(step):
        block = lax.dynamic_index_in_dim(tall, (z + step) % 8, 1, keepdims=False)
        return jnp.dot(block.reshape(2 * rows, width), enc, preferred_element_type=F32)

    up, down = partial(4), partial(-3)
    up, down, tall = lax.optimization_barrier((up, down, tall))
    up, down = lax.ppermute(up, "layer", Z_UP), lax.ppermute(down, "layer", Z_DOWN)
    up, down = up + partial(3), down + partial(-2)
    up, down = lax.ppermute(up, "layer", Z_UP), lax.ppermute(down, "layer", Z_DOWN)
    up, down = up + partial(2), down + partial(-1)
    up, down = lax.ppermute(up, "layer", Z_UP), lax.ppermute(down, "layer", Z_DOWN)
    up = (up + partial(1)).reshape(2, rows, local_latents)
    down = (down + partial(0)).reshape(2, rows, local_latents)

    def column(x, at):
        return lax.dynamic_index_in_dim(x, at, 0, keepdims=False)

    arrived = (
        lax.ppermute(column(up, 1 - x_lo), "layer", Z_ACROSS),
        lax.ppermute(column(up, x_lo), "layer", Z_UP),
        lax.ppermute(column(down, 1 - x_lo), "layer", X_NEXT),
    )
    own_pre = column(down, x_lo) + sum(arrived) + enc_bias[None, :]
    own_latents = jnp.maximum(own_pre, 0.0).astype(BF16)
    latents = spread(own_latents, "layer").reshape(tokens, local_latents)

    acts_rows = lax.dynamic_slice_in_dim(flat, own_half + chip * rows, rows, 0)
    latents, acts_t, acts_rows = lax.optimization_barrier((latents, flat.T, acts_rows))
    flops = 2 * half * local_latents * width
    moved = 2 * (local_latents + half) * width
    halves = shape((half, width), BF16)
    send = simple(send_kernel, halves, flops, moved, core_at, latents, dec)
    received = lax.ppermute(send, "latent", CORE_SWAP)
    chip_sum = simple(keep_kernel, halves, flops, moved, core_at, latents, dec, received)
    shares = lax.all_to_all(
        chip_sum.reshape(8, rows, width), "latent", 0, 0, axis_index_groups=CHIP_GROUPS
    )
    copies = shape((8, rows, width), BF16)
    err_copies = simple(
        functools.partial(error_kernel, scale=math.sqrt(tokens)),
        copies,
        12 * rows * width,
        36 * rows * width,
        shares,
        dec_bias,
        acts_rows,
    )
    err_own = lax.all_to_all(err_copies, "latent", 0, 0, axis_index_groups=CHIP_GROUPS)
    err_own = err_own.reshape(half, width)

    err_other = lax.ppermute(err_own, "latent", CORE_SWAP)
    back = simple(
        back_own_kernel, shape((half, local_latents), BF16), flops, moved, err_own, dec
    )
    back = simple(
        back_kernel,
        shape((tokens, local_latents), BF16),
        flops,
        moved,
        core_at,
        err_other,
        dec,
        back,
    )
    back = back.reshape(2, 8, rows, local_latents)

    def share(step):
        return lax.dynamic_index_in_dim(back, (z + step) % 8, 1, keepdims=False)

    def plus(x, step):
        return x.astype(F32) + share(step).astype(F32)

    up = lax.ppermute(share(4), "layer", Z_UP)
    down = lax.ppermute(share(-3), "layer", Z_DOWN)
    for step in (3, 2):
        up = lax.ppermute(plus(up, step).astype(BF16), "layer", Z_UP)
        down = lax.ppermute(plus(down, 1 - step).astype(BF16), "layer", Z_DOWN)
    up = plus(up, 1).astype(BF16)
    down = plus(down, 0)
    arrived = (
        lax.ppermute(column(up, 1 - x_lo), "layer", Z_ACROSS),
        lax.ppermute(column(up, x_lo), "layer", Z_UP),
        lax.ppermute(column(down.astype(BF16), 1 - x_lo), "layer", X_NEXT),
    )
    latent_grad = column(down, x_lo) + sum(x.astype(F32) for x in arrived)
    own_grad_pre = jnp.where(own_pre > 0, latent_grad, 0.0).astype(BF16)
    third = width // 3
    dec_grad = call(
        dec_kernel,
        shape((local_latents, width), BF16),
        pl.BlockSpec((local_latents, third), lambda i: (0, i)),
        [
            SMALL,
            whole(latents),
            pl.BlockSpec((half, third), lambda i: (0, i)),
            pl.BlockSpec((half, third), lambda i: (0, i)),
        ],
        2 * flops,
        3 * moved,
        core_at,
        latents,
        err_own,
        err_other,
        steps=3,
    )
    own_grad_pre, dec_grad = lax.optimization_barrier((own_grad_pre, dec_grad))
    grad_pre = spread(own_grad_pre, "layer").reshape(tokens, local_latents)
    by_rows = pl.BlockSpec((width // 2, local_latents), lambda i: (i, 0))
    enc_grad = call(
        enc_kernel,
        shape((width, local_latents), BF16),
        by_rows,
        [pl.BlockSpec((width // 2, tokens), lambda i: (i, 0)), whole(grad_pre)],
        2 * flops,
        3 * moved,
        acts_t,
        grad_pre,
        steps=2,
    )
    return (
        latent_grad,
        enc_grad.reshape(layers_here, width, local_latents),
        dec_grad.reshape(local_latents, layers_here, width),
    )


def solution(mesh):
    in_specs = (
        P(None, "layer", None),
        P("layer", None, "latent"),
        P("latent", "layer", None),
        P("latent"),
        P("layer", None),
    )
    out_specs = (P("layer", "latent"), P("layer", None, "latent"), P("latent", "layer", None))
    return jax.shard_map(local, mesh=mesh, in_specs=in_specs, out_specs=out_specs, check_vma=False)
```

```python
import functools
import math

import jax
import jax.numpy as jnp
from jax import lax
from jax.experimental import pallas as pl
from jax.experimental.pallas import tpu as pltpu
from jax.sharding import PartitionSpec as P

F32 = jnp.float32
BF16 = jnp.bfloat16
CORE_SWAP = [(i, i ^ 1) for i in range(16)]
CHIP_GROUPS = [list(range(c, 16, 2)) for c in range(2)]


Z_UP = [(x * 8 + z, x * 8 + (z + 1) % 8) for x in range(2) for z in range(8)]
Z_DOWN = [(b, a) for a, b in Z_UP]
Z_ACROSS = [(a, b ^ 8) for a, b in Z_UP]
X_NEXT = [(i, (i + 8) % 16) for i in range(16)]


def spread(block, axis, groups=None, count=16):
    copies = jnp.broadcast_to(block[None], (count,) + block.shape)
    return lax.all_to_all(copies, axis, 0, 0, axis_index_groups=groups)


SMALL = pl.BlockSpec(memory_space=pltpu.SMEM)
NT = (((1,), (1,)), ((), ()))
TN = (((0,), (0,)), ((), ()))


def shape(dims, dtype):
    return jax.ShapeDtypeStruct(dims, dtype)


def whole(like):
    if like.shape == (1,):
        return SMALL
    return pl.BlockSpec(like.shape, lambda i: (0,) * len(like.shape))


def simple(kernel, out_shape, flops, moved, *operands):
    specs = [whole(operand) for operand in operands]
    return call(kernel, out_shape, whole(out_shape), specs, flops, moved, *operands)


def call(kernel, out_shape, out_spec, specs, flops, moved, *operands, steps=1):
    return pl.pallas_call(
        kernel,
        out_shape=out_shape,
        grid=(steps,),
        in_specs=specs,
        out_specs=out_spec,
        compiler_params=pltpu.CompilerParams(vmem_limit_bytes=20 * 1024 * 1024),
        cost_estimate=pl.CostEstimate(flops=flops, bytes_accessed=moved, transcendentals=0),
    )(*operands)


def error_kernel(shares_ref, bias_ref, acts_ref, copies_ref, *, scale):
    recon = shares_ref[0].astype(F32)
    for i in range(1, shares_ref.shape[0]):
        recon += shares_ref[i].astype(F32)
    err = (recon + bias_ref[...] - acts_ref[...].astype(F32)) / scale
    err = err.astype(BF16)
    for i in range(copies_ref.shape[0]):
        copies_ref[i] = err


def half_of(ref, which):
    rows = ref.shape[0] // 2
    return ref[pl.ds(pl.multiple_of(which * rows, rows), rows), :]


def send_kernel(core_ref, latents_ref, dec_ref, out_ref):
    left = half_of(latents_ref, 1 - core_ref[0])
    out_ref[...] = jnp.dot(left, dec_ref[...], preferred_element_type=F32).astype(BF16)


def keep_kernel(core_ref, latents_ref, dec_ref, received_ref, out_ref):
    left = half_of(latents_ref, core_ref[0])
    total = jnp.dot(left, dec_ref[...], preferred_element_type=F32)
    out_ref[...] = (total + received_ref[...].astype(F32)).astype(BF16)


def back_own_kernel(err_ref, dec_ref, out_ref):
    out_ref[...] = lax.dot_general(
        err_ref[...], dec_ref[...], NT, preferred_element_type=F32
    ).astype(BF16)


def back_kernel(core_ref, err_ref, dec_ref, own_ref, out_ref):
    half = err_ref.shape[0]
    core = core_ref[0]
    other = lax.dot_general(err_ref[...], dec_ref[...], NT, preferred_element_type=F32)
    out_ref[pl.ds(pl.multiple_of(core * half, half), half), :] = own_ref[...]
    out_ref[pl.ds(pl.multiple_of((1 - core) * half, half), half), :] = other.astype(BF16)


def dec_kernel(core_ref, latents_ref, own_ref, other_ref, out_ref):
    core = core_ref[0]
    total = lax.dot_general(
        half_of(latents_ref, core), own_ref[...], TN, preferred_element_type=F32
    )
    total += lax.dot_general(
        half_of(latents_ref, 1 - core), other_ref[...], TN, preferred_element_type=F32
    )
    out_ref[...] = total.astype(BF16)


def enc_kernel(acts_ref, grad_ref, out_ref):
    out_ref[...] = jnp.dot(
        acts_ref[...], grad_ref[...], preferred_element_type=F32
    ).astype(BF16)


def local(acts, enc_weight, dec_weight, enc_bias, dec_bias):
    tokens, layers_here, width = acts.shape
    local_latents = enc_weight.shape[2]
    flat = acts.reshape(tokens, width)
    enc = enc_weight.reshape(width, local_latents)
    dec = dec_weight.reshape(local_latents, width)
    rows = tokens // 16
    half = tokens // 2
    core = lax.axis_index("latent") % 2
    chip = lax.axis_index("latent") // 2
    core_at = core.reshape(1)
    own_half = core * half
    other_half = (1 - core) * half

    layer_at = lax.axis_index("layer")
    x_lo = layer_at // 8
    z = layer_at % 8
    tall = flat.reshape(2, 8, rows, width)

    def partial(step):
        block = lax.dynamic_index_in_dim(tall, (z + step) % 8, 1, keepdims=False)
        return jnp.dot(block.reshape(2 * rows, width), enc, preferred_element_type=F32)

    up, tall = lax.optimization_barrier((partial(4), tall))
    down = partial(-3)
    up, down = lax.ppermute(up, "layer", Z_UP), lax.ppermute(down, "layer", Z_DOWN)
    up, down = up + partial(3), down + partial(-2)
    up, down = lax.ppermute(up, "layer", Z_UP), lax.ppermute(down, "layer", Z_DOWN)
    up, down = up + partial(2), down + partial(-1)
    up, down = lax.ppermute(up, "layer", Z_UP), lax.ppermute(down, "layer", Z_DOWN)
    up = (up + partial(1)).reshape(2, rows, local_latents)
    down = (down + partial(0)).reshape(2, rows, local_latents)

    def column(x, at):
        return lax.dynamic_index_in_dim(x, at, 0, keepdims=False)

    arrived = (
        lax.ppermute(column(up, 1 - x_lo), "layer", Z_ACROSS),
        lax.ppermute(column(up, x_lo), "layer", Z_UP),
        lax.ppermute(column(down, 1 - x_lo), "layer", X_NEXT),
    )
    own_pre = column(down, x_lo) + sum(arrived) + enc_bias[None, :]
    own_latents = jnp.maximum(own_pre, 0.0).astype(BF16)
    latents = spread(own_latents, "layer").reshape(tokens, local_latents)

    acts_rows = lax.dynamic_slice_in_dim(flat, own_half + chip * rows, rows, 0)
    latents, acts_t, acts_rows = lax.optimization_barrier((latents, flat.T, acts_rows))
    flops = 2 * half * local_latents * width
    moved = 2 * (local_latents + half) * width
    halves = shape((half, width), BF16)
    send = simple(send_kernel, halves, flops, moved, core_at, latents, dec)
    received = lax.ppermute(send, "latent", CORE_SWAP)
    chip_sum = simple(keep_kernel, halves, flops, moved, core_at, latents, dec, received)
    shares = lax.all_to_all(
        chip_sum.reshape(8, rows, width), "latent", 0, 0, axis_index_groups=CHIP_GROUPS
    )
    copies = shape((8, rows, width), BF16)
    err_copies = simple(
        functools.partial(error_kernel, scale=math.sqrt(tokens)),
        copies,
        12 * rows * width,
        36 * rows * width,
        shares,
        dec_bias,
        acts_rows,
    )
    err_own = lax.all_to_all(err_copies, "latent", 0, 0, axis_index_groups=CHIP_GROUPS)
    err_own = err_own.reshape(half, width)

    err_other = lax.ppermute(err_own, "latent", CORE_SWAP)
    back = simple(
        back_own_kernel, shape((half, local_latents), BF16), flops, moved, err_own, dec
    )
    back = simple(
        back_kernel,
        shape((tokens, local_latents), BF16),
        flops,
        moved,
        core_at,
        err_other,
        dec,
        back,
    )
    back = back.reshape(2, 8, rows, local_latents)

    def share(step):
        return lax.dynamic_index_in_dim(back, (z + step) % 8, 1, keepdims=False)

    def plus(x, step):
        return x.astype(F32) + share(step).astype(F32)

    up = lax.ppermute(share(4), "layer", Z_UP)
    down = lax.ppermute(share(-3), "layer", Z_DOWN)
    for step in (3, 2):
        up = lax.ppermute(plus(up, step).astype(BF16), "layer", Z_UP)
        down = lax.ppermute(plus(down, 1 - step).astype(BF16), "layer", Z_DOWN)
    up = plus(up, 1).astype(BF16)
    down = plus(down, 0)
    arrived = (
        lax.ppermute(column(up, 1 - x_lo), "layer", Z_ACROSS),
        lax.ppermute(column(up, x_lo), "layer", Z_UP),
        lax.ppermute(column(down.astype(BF16), 1 - x_lo), "layer", X_NEXT),
    )
    latent_grad = column(down, x_lo) + sum(x.astype(F32) for x in arrived)
    own_grad_pre = jnp.where(own_pre > 0, latent_grad, 0.0).astype(BF16)
    third = width // 3
    dec_grad = call(
        dec_kernel,
        shape((local_latents, width), BF16),
        pl.BlockSpec((local_latents, third), lambda i: (0, i)),
        [
            SMALL,
            whole(latents),
            pl.BlockSpec((half, third), lambda i: (0, i)),
            pl.BlockSpec((half, third), lambda i: (0, i)),
        ],
        2 * flops,
        3 * moved,
        core_at,
        latents,
        err_own,
        err_other,
        steps=3,
    )
    own_grad_pre, dec_grad = lax.optimization_barrier((own_grad_pre, dec_grad))
    grad_pre = spread(own_grad_pre, "layer").reshape(tokens, local_latents)
    by_rows = pl.BlockSpec((width // 2, local_latents), lambda i: (i, 0))
    enc_grad = call(
        enc_kernel,
        shape((width, local_latents), BF16),
        by_rows,
        [pl.BlockSpec((width // 2, tokens), lambda i: (i, 0)), whole(grad_pre)],
        2 * flops,
        3 * moved,
        acts_t,
        grad_pre,
        steps=2,
    )
    return (
        latent_grad,
        enc_grad.reshape(layers_here, width, local_latents),
        dec_grad.reshape(local_latents, layers_here, width),
    )


def solution(mesh):
    in_specs = (
        P(None, "layer", None),
        P("layer", None, "latent"),
        P("latent", "layer", None),
        P("latent"),
        P("layer", None),
    )
    out_specs = (P("layer", "latent"), P("layer", None, "latent"), P("latent", "layer", None))
    return jax.shard_map(local, mesh=mesh, in_specs=in_specs, out_specs=out_specs, check_vma=False)
```
